32 devices in a mesh: groups: 2 (over x), gx: 8 (over z, y), gy: 2 (over core).
Axes of the slice: x: 2, y: 2, z: 4, core: 2. Of those that a mesh axis runs over, the one named last changes fastest.
Arguments:
- hidden: bfloat16 [256, 2, 16384], P(('groups', 'gy'), None, 'gx'), parts along dimension 0, may hold values from -60 to 60
- norm_gain: bfloat16 [16384], P('gx'), may hold values from 0.099609375 to 1.8984375
- w_query: bfloat16 [16384, 8192], P('gx', 'gy'), may hold values from -0.5 to 0.5
- key_weight: bfloat16 [16384, 512], P('gx', 'gy'), may hold values from -0.5 to 0.5
- value_weight: bfloat16 [16384, 512], P('gx', 'gy'), may hold values from -0.046875 to 0.046875
- w_out: bfloat16 [8192, 16384], P('gy', 'gx'), may hold values from -0.0625 to 0.0625
- stored_rotated_keys: bfloat16 [256, 1024, 512], P(('groups', 'gx', 'gy')), parts along dimension 0, may hold values from -1240 to 1240
- stored_value_rows: bfloat16 [256, 1024, 512], P(('groups', 'gx', 'gy')), parts along dimension 0, may hold values from -10 to 10
- lengths: int32 [256], P(('groups', 'gx', 'gy')), parts along dimension 0, may hold values from 1 to 1024, 65536 in all
Outputs:
- branch_out: bfloat16 [256, 2, 16384], P(('groups', 'gy'), None, 'gx'), parts along dimension 0
The draws below stay inside these ranges and needn't reach their ends.
There are 2 independent parts, one for each index of `groups`. The reference program is written for one: setup_inputs(seed, part) draws one part's arguments, and reference() takes and returns one part's arrays. A program takes and returns all parts, laid end to end along the dimension named above; an argument that names none is the same for every part. Nothing has to cross between parts.
Inputs may be any that keep to these rules, and one draw needn't show every extreme that they name: Cache positions below a row's length are live; the lengths of one group sum to 65536; some row's length is 1024.
All inputs are finite; a program needn't handle non-finite values.
Results may differ from the reference program's by a relative error of at most 0.008.
Values may be sent and summed in bfloat16 or wider, within the bound.
A program may use at most 128 MiB of HBM per device.

```python
import math
import jax
import jax.numpy as jnp
import numpy as np
from jax import lax

MODEL_WIDTH = 16384
QUERY_HEADS = 64
KEY_VALUE_HEADS = 4
HEAD_SIZE = 128
STEPS = 2
CACHE_SLOTS = 1024
GROUP_ROWS = 128


def common_columns(key):
    return jnp.clip(jax.random.normal(key, (MODEL_WIDTH, KEY_VALUE_HEADS * HEAD_SIZE), jnp.float32), -4.0, 4.0)


def draw_w_query(key, part):
    shared = common_columns(key)
    key = jax.random.fold_in(key, 31)
    private = jnp.clip(jax.random.normal(key, (MODEL_WIDTH, QUERY_HEADS * HEAD_SIZE), jnp.float32), -4.0, 4.0)
    widened = jnp.broadcast_to(shared.reshape(MODEL_WIDTH, KEY_VALUE_HEADS, 1, HEAD_SIZE), (MODEL_WIDTH, KEY_VALUE_HEADS, QUERY_HEADS // KEY_VALUE_HEADS, HEAD_SIZE))
    widened = widened.reshape(MODEL_WIDTH, QUERY_HEADS * HEAD_SIZE)
    return ((math.sqrt(0.45) * widened + math.sqrt(0.55) * private) / math.sqrt(MODEL_WIDTH)).astype(jnp.bfloat16)


def draw_key_weight(key, part):
    shared = common_columns(key)
    key = jax.random.fold_in(key, 37)
    private = jnp.clip(jax.random.normal(key, (MODEL_WIDTH, KEY_VALUE_HEADS * HEAD_SIZE), jnp.float32), -4.0, 4.0)
    return ((math.sqrt(0.45) * shared + math.sqrt(0.55) * private) / math.sqrt(MODEL_WIDTH)).astype(jnp.bfloat16)


def draw_hidden(key, part):
    key = jax.random.fold_in(key, 11)
    key_base, key_rows, key_cols = jax.random.split(key, 3)
    array_shape = (GROUP_ROWS, STEPS, MODEL_WIDTH)
    base = jnp.clip(jax.random.normal(key_base, array_shape, jnp.float32), -4.0, 4.0)
    row_scale = jnp.exp(jax.random.uniform(key_rows, (GROUP_ROWS, STEPS, 1), jnp.float32, math.log(0.3), math.log(3.0)))
    column_scale = jnp.exp(jax.random.uniform(key_cols, (MODEL_WIDTH,), jnp.float32, -1.15, 1.15))
    ramp_scale = jnp.sqrt(0.6 + 1.2 * jnp.arange(MODEL_WIDTH, dtype=jnp.float32) / MODEL_WIDTH)
    return (base * row_scale * column_scale * ramp_scale).astype(jnp.bfloat16)


def draw_stored_rotated_keys(key, part):
    key = jax.random.fold_in(key, 23)
    key_base = jax.random.fold_in(key, 0)
    array_shape = (GROUP_ROWS, CACHE_SLOTS, KEY_VALUE_HEADS * HEAD_SIZE)
    base = jnp.clip(jax.random.normal(key_base, array_shape, jnp.float32), -5.0, 5.0)
    return base.astype(jnp.bfloat16)


def levels(own_key, dims, pieces, smallest, largest):
    loudness, own = 1.0, jax.random.fold_in(own_key, 6)
    for dim, blocks in pieces:
        draws = jnp.exp(jax.random.uniform(jax.random.fold_in(own, dim), (blocks,), jnp.float32, smallest / len(pieces), largest / len(pieces)))
        loudness = loudness * jnp.repeat(draws, dims[dim] // blocks).reshape([-1 if axis == dim else 1 for axis in range(len(dims))])
    return loudness


def profile(amount, total, limit, slope):
    loads = [(1 << 20) // math.isqrt(rank ** slope) + 1 for rank in range(2, amount + 1)]
    spare, given = total - limit - (amount - 1), [1] * (amount - 1)
    while spare > 0:
        candidates = [i for i in range(amount - 1) if given[i] < limit]
        pool, left = sum([loads[i] for i in candidates]), spare
        for i in candidates:
            extra = min(limit - given[i], max(1, left * loads[i] // pool), spare)
            given[i] = given[i] + extra
            spare = spare - extra
    return np.array([limit] + given)


def ragged_sizes(key, number_of, total, limit, slope):
    if number_of == 2:
        one = jax.random.randint(key, (), max(1, total - limit), min(limit, total - 1) + 1)
        return jnp.stack([one, total - one])
    sizes = jnp.asarray(profile(number_of, total, limit, slope), jnp.int32)
    pairs = (number_of - 1) // 2
    donor, receiver = sizes[1:1 + 2 * pairs:2], sizes[2:2 + 2 * pairs:2]
    margin = jnp.minimum(donor - 1, limit - receiver)
    moved = jax.random.randint(jax.random.fold_in(key, 1), (pairs,), 0, 1 << 20) % (margin + 1)
    sizes = sizes.at[1:1 + 2 * pairs:2].set(donor - moved).at[2:2 + 2 * pairs:2].set(receiver + moved)
    return sizes[jax.random.permutation(jax.random.fold_in(key, 2), number_of)]


def centred(rng, shape, scale, most, shards=(), kind=jnp.bfloat16):
    gain = levels(rng, shape, shards, -0.22, 0.18) if shards else 1.0
    values = jax.random.normal(rng, shape, jnp.float32) * scale * gain
    return jnp.minimum(jnp.maximum(values, -most), most).astype(kind)


def setup_inputs(seed: int = 0, part: int = 0) -> dict:
    streams_of = jax.random.split(jax.random.key(seed), 10)
    part_splits = jax.random.split(jax.random.fold_in(streams_of[9], part), 10)
    return {
        "hidden": draw_hidden(jax.random.fold_in(jax.random.fold_in(streams_of[9], part), 71), part),
        "norm_gain": jnp.clip(1.0 + 0.18 * jax.random.normal(streams_of[1], (MODEL_WIDTH,), jnp.float32), 0.099609375, 1.8984375).astype(jnp.bfloat16),
        "w_query": draw_w_query(jax.random.fold_in(streams_of[9], 71), part),
        "key_weight": draw_key_weight(jax.random.fold_in(streams_of[9], 71), part),
        "value_weight": centred(streams_of[4], (MODEL_WIDTH, KEY_VALUE_HEADS * HEAD_SIZE), MODEL_WIDTH ** -0.5, 0.046875, ((0, 8), (1, 2))),
        "w_out": centred(streams_of[5], (QUERY_HEADS * HEAD_SIZE, MODEL_WIDTH), (QUERY_HEADS * HEAD_SIZE) ** -0.5, 0.0625, ((0, 2), (1, 8))),
        "stored_rotated_keys": draw_stored_rotated_keys(jax.random.fold_in(jax.random.fold_in(streams_of[9], part), 71), part),
        "stored_value_rows": centred(part_splits[7], (GROUP_ROWS, CACHE_SLOTS, KEY_VALUE_HEADS * HEAD_SIZE), 2.0, 10.0, ((0, 16),)),
        "lengths": ragged_sizes(part_splits[8], GROUP_ROWS, GROUP_ROWS * CACHE_SLOTS // 2, CACHE_SLOTS, 1).astype(jnp.int32),
    }


epsilon = 1e-05
rope_base = 500000.0

def rotary_embed(inputs, token_positions):
    half_dim = inputs.shape[-1] // 2
    frequency = rope_base ** (-jnp.arange(half_dim, dtype=jnp.float32) / half_dim)
    angles = token_positions.astype(jnp.float32)[..., None, None] * frequency
    cosine = jnp.cos(angles)
    sine_part = jnp.sin(angles)
    lower_half = inputs[..., :half_dim]
    upper_half = inputs[..., half_dim:]
    return jnp.concatenate([lower_half * cosine - upper_half * sine_part, upper_half * cosine + lower_half * sine_part], axis=-1)

def reference(hidden, norm_gain, w_query, key_weight, value_weight, w_out, stored_rotated_keys, stored_value_rows, lengths):
    queries_per_group = QUERY_HEADS // KEY_VALUE_HEADS
    inverse = 1.0 / math.sqrt(HEAD_SIZE)
    cached_key_rows = stored_rotated_keys.astype(jnp.float32).reshape(GROUP_ROWS, CACHE_SLOTS, KEY_VALUE_HEADS, HEAD_SIZE)
    cached_value_rows = stored_value_rows.astype(jnp.float32).reshape(GROUP_ROWS, CACHE_SLOTS, KEY_VALUE_HEADS, HEAD_SIZE)
    live_mask = jnp.arange(CACHE_SLOTS)[None, :] < lengths[:, None]
    key_list = []
    collected_values = []
    outputs = []
    for step_index in range(STEPS):
        widened = hidden[:, step_index].astype(jnp.float32)
        factor = lax.rsqrt(lax.optimization_barrier(jnp.mean(widened * widened, axis=-1, keepdims=True)) + epsilon)
        normed = (widened * factor * norm_gain.astype(jnp.float32)).astype(jnp.bfloat16)
        query_rows = jnp.dot(normed, w_query, preferred_element_type=jnp.float32).astype(jnp.bfloat16)
        unrotated_keys = jnp.dot(normed, key_weight, preferred_element_type=jnp.float32).astype(jnp.bfloat16)
        fresh_values = jnp.dot(normed, value_weight, preferred_element_type=jnp.float32).astype(jnp.bfloat16)
        token_positions = lengths + step_index
        query_rows = rotary_embed(query_rows.astype(jnp.float32).reshape(GROUP_ROWS, QUERY_HEADS, HEAD_SIZE), token_positions).astype(jnp.bfloat16)
        fresh_keys = rotary_embed(unrotated_keys.astype(jnp.float32).reshape(GROUP_ROWS, KEY_VALUE_HEADS, HEAD_SIZE), token_positions).astype(jnp.bfloat16)
        key_list.append(fresh_keys)
        collected_values.append(fresh_values.reshape(GROUP_ROWS, KEY_VALUE_HEADS, HEAD_SIZE))
        stacked_k = jnp.stack(key_list, axis=1).astype(jnp.float32)
        stacked_v = jnp.stack(collected_values, axis=1).astype(jnp.float32)
        grouped_queries = query_rows.astype(jnp.float32).reshape(GROUP_ROWS, KEY_VALUE_HEADS, queries_per_group, HEAD_SIZE)
        score_cache = jnp.einsum('rgqd,rlgd->rgql', grouped_queries, cached_key_rows) * inverse
        score_cache = jnp.where(live_mask[:, None, None, :], score_cache, -jnp.inf)
        score_new = jnp.einsum('rgqd,rsgd->rgqs', grouped_queries, stacked_k) * inverse
        highest = jnp.maximum(lax.optimization_barrier(jnp.max(score_cache, axis=-1)), lax.optimization_barrier(jnp.max(score_new, axis=-1)))
        exp_cache = jnp.exp(score_cache - highest[..., None])
        exp_new = jnp.exp(score_new - highest[..., None])
        denominator = lax.optimization_barrier(jnp.sum(exp_cache, axis=-1)) + lax.optimization_barrier(jnp.sum(exp_new, axis=-1))
        weight_cache = (exp_cache / denominator[..., None]).astype(jnp.bfloat16)
        weight_new = (exp_new / denominator[..., None]).astype(jnp.bfloat16)
        attended = jnp.einsum('rgql,rlgd->rgqd', weight_cache.astype(jnp.float32), cached_value_rows)
        attended = attended + jnp.einsum('rgqs,rsgd->rgqd', weight_new.astype(jnp.float32), stacked_v)
        attended = attended.astype(jnp.bfloat16).reshape(GROUP_ROWS, QUERY_HEADS * HEAD_SIZE)
        outputs.append(jnp.dot(attended, w_out, preferred_element_type=jnp.float32).astype(jnp.bfloat16))
    return jnp.stack(outputs, axis=1)
```

```python
import functools
import math

import jax
import jax.numpy as jnp
from jax import lax
from jax.experimental import pallas as pl
from jax.experimental.pallas import tpu as pltpu
from jax.sharding import PartitionSpec as P

HEAD_SIZE = 128
CHUNK = 512
WIRE = jnp.int16
SMALL = 2.0**-20
CODES = 32767.0 / math.log(2.0**34.5)
epsilon = 1e-05
rope_base = 500000.0


def encode(values):
    size = jnp.log(1.0 + jnp.abs(values) * (1.0 / SMALL)) * CODES + 0.5
    return jnp.where(values < 0, -size, size).astype(jnp.int32).astype(WIRE)


def decode(codes):
    wide = codes.astype(jnp.int32).astype(jnp.float32)
    size = jnp.exp(jnp.abs(wide) * (1.0 / CODES)) * SMALL - SMALL
    return jnp.where(wide < 0, -size, size)


def remote(src, dst, send, recv, device):
    return pltpu.make_async_remote_copy(
        src_ref=src,
        dst_ref=dst,
        send_sem=send,
        recv_sem=recv,
        device_id=device,
        device_id_type=pl.DeviceIdType.MESH,
    )


def position(gx_count):
    gx = lax.axis_index("gx")
    core = lax.axis_index("gy")
    depth = gx_count // 2
    far, near = gx // 2, lax.rem(gx, 2)
    sibling = {"gy": 1 - core}
    pair = {"gx": far * 2 + (1 - near)}

    def line(d):
        return {"gx": lax.rem(far + d, depth) * 2 + near}

    return core, far, near, sibling, pair, line


def greet(sibling, pair, line, depth):
    barrier = pltpu.get_barrier_semaphore()
    devices = [sibling, pair] + [line(d) for d in range(1, depth)]
    for device in devices:
        pl.semaphore_signal(
            barrier, inc=1, device_id=device, device_id_type=pl.DeviceIdType.MESH
        )
    pl.semaphore_wait(barrier, len(devices))


def project_kernel(
    gx_count,
    rows_block,
    x_ref,
    gain_ref,
    wq_ref,
    kw_ref,
    vw_ref,
    out_ref,
    wbuf,
    xs,
    mine,
    mid,
    pair_sums,
    line_sums,
    normed,
    own,
    s1,
    r1,
    s2,
    r2,
    fin,
    fin_in,
    wsem,
    xsem,
    psem,
    lsem,
    s1s,
    s1r,
    s2s,
    s2r,
    fsem,
):
    depth = gx_count // 2
    chunks, width, _ = wbuf.shape
    half_rows = xs.shape[1]
    rows = 2 * half_rows
    key_width = kw_ref.shape[1]
    core, far, near, sibling, pair, line = position(gx_count)

    def load_query(c):
        return pltpu.make_async_copy(
            wq_ref.at[:, pl.ds(pl.multiple_of(c * CHUNK, CHUNK), CHUNK)],
            wbuf.at[c],
            wsem.at[c],
        )

    load_key = pltpu.make_async_copy(
        kw_ref, wbuf.at[chunks - 1, :, pl.ds(0, key_width)], wsem.at[chunks - 1]
    )
    load_value = pltpu.make_async_copy(
        vw_ref, wbuf.at[chunks - 1, :, pl.ds(key_width, key_width)], wsem.at[chunks]
    )

    @pl.loop(0, chunks - 1)
    def _(c):
        load_query(c).start()

    load_key.start()
    load_value.start()
    greet(sibling, pair, line, depth)

    send_x = remote(x_ref, xs.at[core], xsem.at[0], xsem.at[1], sibling)
    send_x.start()
    xs[core] = x_ref[...]
    send_x.wait()

    columns = []
    for g in range(2):
        wide = xs[g].astype(jnp.float32)
        columns.append(jnp.sum(wide * wide, axis=1, keepdims=True))
    column = jnp.concatenate(columns, axis=0)
    mine[...] = jnp.transpose(jnp.broadcast_to(column, (rows, 128)))[0:8, :]
    swap = remote(mine, pair_sums, psem.at[0], psem.at[1], pair)
    swap.start()
    swap.wait()
    mid[...] = mine[...] + pair_sums[...]
    line_copies = [
        remote(mid, line_sums.at[d], lsem.at[0, d], lsem.at[1, d], line(d))
        for d in range(1, depth)
    ]
    for copy in line_copies:
        copy.start()
    for copy in line_copies:
        copy.wait()
    total = mid[...]
    for d in range(1, depth):
        total = total + line_sums[d]
    factor_row = lax.rsqrt(total * (1.0 / (width * gx_count)) + epsilon)
    factor = jnp.transpose(jnp.broadcast_to(factor_row[0:1, :], (128, rows)))[:, 0:1]
    gain = gain_ref[...].astype(jnp.float32)
    blocks_half = half_rows // rows_block
    for b in range(2 * blocks_half):
        start = (b % blocks_half) * rows_block
        wide = xs[b // blocks_half, start : start + rows_block, :].astype(jnp.float32)
        scaled = wide * factor[b * rows_block : (b + 1) * rows_block, :] * gain
        normed[(b % 2) * depth + b // 2] = scaled.astype(jnp.bfloat16)

    def first(c):
        return remote(s1.at[c], r1.at[c], s1s.at[c], s1r.at[c], pair)

    def second(c, d):
        return remote(
            s2.at[c, lax.rem(far + d, depth)], r2.at[c, d], s2s.at[c, d], s2r.at[c, d], line(d)
        )

    lag = 2

    @pl.loop(0, chunks + lag)
    def _(c):
        @pl.when(c < chunks)
        def _():
            @pl.when(c < chunks - 1)
            def _():
                load_query(c).wait()

            @pl.when(c == chunks - 1)
            def _():
                load_key.wait()
                load_value.wait()

            part = jnp.dot(
                normed[...].reshape(rows, width), wbuf[c], preferred_element_type=jnp.float32
            ).reshape(2, depth, rows_block, CHUNK)

            @pl.when(near == 0)
            def _():
                own[c] = part[0]
                s1[c] = encode(part[1])

            @pl.when(near == 1)
            def _():
                own[c] = part[1]
                s1[c] = encode(part[0])

            first(c).start()

        @pl.when(c >= lag)
        def _():
            cc = c - lag
            first(cc).wait_recv()
            both = own[cc] + decode(r1[cc])
            own[cc] = both
            s2[cc] = encode(both)
            for d in range(1, depth):
                second(cc, d).start()

    @pl.loop(0, chunks)
    def _(c):
        summed = own[c, far]
        for d in range(1, depth):
            second(c, d).wait_recv()
            summed = summed + decode(r2[c, d])
        rounded = summed.astype(jnp.bfloat16)
        for g in range(2):
            fin[g, c] = rounded[g * (rows_block // 2) : (g + 1) * (rows_block // 2), :]

    last = remote(fin.at[1 - core], fin_in, fsem.at[0], fsem.at[1], sibling)
    last.start()
    out_ref[core] = fin[core]

    @pl.loop(0, chunks)
    def _(c):
        first(c).wait_send()
        for d in range(1, depth):
            second(c, d).wait_send()

    last.wait()
    out_ref[1 - core] = fin_in[...]


def project(x, gain, w_query, key_weight, value_weight, gx_count):
    half_rows, width = x.shape
    rows = 2 * half_rows
    rows_block = rows // gx_count
    depth = gx_count // 2
    chunks = w_query.shape[1] // CHUNK + 1
    out_rows = rows_block // 2
    vmem = pl.BlockSpec(memory_space=pltpu.VMEM)
    hbm = pl.BlockSpec(memory_space=pl.ANY)
    dma = pltpu.SemaphoreType.DMA
    return pl.pallas_call(
        functools.partial(project_kernel, gx_count, rows_block),
        out_shape=jax.ShapeDtypeStruct((2, chunks, out_rows, CHUNK), jnp.bfloat16),
        in_specs=[vmem, vmem, hbm, hbm, hbm],
        out_specs=vmem,
        scratch_shapes=[
            pltpu.VMEM((chunks, width, CHUNK), jnp.bfloat16),
            pltpu.VMEM((2, half_rows, width), jnp.bfloat16),
            pltpu.VMEM((8, rows), jnp.float32),
            pltpu.VMEM((8, rows), jnp.float32),
            pltpu.VMEM((8, rows), jnp.float32),
            pltpu.VMEM((depth, 8, rows), jnp.float32),
            pltpu.VMEM((2 * depth, rows_block, width), jnp.bfloat16),
            pltpu.VMEM((chunks, depth, rows_block, CHUNK), jnp.float32),
            pltpu.VMEM((chunks, depth, rows_block, CHUNK), WIRE),
            pltpu.VMEM((chunks, depth, rows_block, CHUNK), WIRE),
            pltpu.VMEM((chunks, depth, rows_block, CHUNK), WIRE),
            pltpu.VMEM((chunks, depth, rows_block, CHUNK), WIRE),
            pltpu.VMEM((2, chunks, out_rows, CHUNK), jnp.bfloat16),
            pltpu.VMEM((chunks, out_rows, CHUNK), jnp.bfloat16),
            dma((chunks + 1,)),
            dma((2,)),
            dma((2,)),
            dma((2, depth)),
            dma((chunks,)),
            dma((chunks,)),
            dma((chunks, depth)),
            dma((chunks, depth)),
            dma((2,)),
        ],
        compiler_params=pltpu.CompilerParams(
            collective_id=1, has_side_effects=True, vmem_limit_bytes=56 * 1024 * 1024
        ),
    )(x, gain, w_query, key_weight, value_weight)


def output_kernel(
    gx_count,
    att_ref,
    w_ref,
    out_ref,
    wbuf,
    full,
    acc,
    acc_in,
    wsem,
    gsem,
    zs,
    zr,
    ys,
    yr,
    fsem,
):
    depth = gx_count // 2
    chunks = wbuf.shape[0]
    width = wbuf.shape[2]
    _, _, _, _, half, _ = full.shape
    rows = 2 * depth * 2 * half
    core, far, near, sibling, pair, line = position(gx_count)

    def load(c):
        return pltpu.make_async_copy(
            w_ref.at[pl.ds(pl.multiple_of(c * CHUNK, CHUNK), CHUNK), :], wbuf.at[c], wsem.at[c]
        )

    @pl.loop(0, chunks)
    def _(c):
        load(c).start()

    greet(sibling, pair, line, depth)
    give = remote(
        att_ref.at[1 - core],
        full.at[:, near, far, core],
        gsem.at[0],
        gsem.at[1],
        sibling,
    )
    give.start()

    @pl.loop(0, chunks)
    def _(c):
        full[c, near, far, core] = att_ref[core, c]

    acc[...] = jnp.zeros_like(acc)
    give.wait()

    def along(c, d):
        block = full.at[c, near, far]
        return remote(block, block, zs.at[c, d], zr.at[c, d], line(d))

    def across(c, d):
        block = full.at[c, near, lax.rem(far + depth - d, depth)]
        return remote(block, block, ys.at[c, d], yr.at[c, d], pair)

    @pl.loop(0, chunks)
    def _(c):
        across(c, 0).start()
        for d in range(1, depth):
            along(c, d).start()

    lag = 1

    @pl.loop(0, chunks + lag)
    def _(c):
        @pl.when(c < chunks)
        def _():
            for d in range(1, depth):
                along(c, d).wait_recv()
                across(c, d).start()

        @pl.when(c >= lag)
        def _():
            cc = c - lag
            for d in range(depth):
                across(cc, d).wait_recv()
            load(cc).wait()
            acc[...] += jnp.dot(
                full[cc].reshape(rows, CHUNK), wbuf[cc], preferred_element_type=jnp.float32
            ).reshape(2, depth, 2 * half, width)

    keep = depth // 2
    last = remote(
        acc.at[:, pl.ds((1 - core) * keep, keep)], acc_in, fsem.at[0], fsem.at[1], sibling
    )
    last.start()

    @pl.loop(0, chunks)
    def _(c):
        across(c, 0).wait_send()
        for d in range(1, depth):
            along(c, d).wait_send()
            across(c, d).wait_send()

    last.wait()
    for z in range(keep):
        for y in range(2):
            out_ref[z, y] = (acc[y, core * keep + z] + acc_in[y, z]).astype(out_ref.dtype)


def output(attended, w_out, gx_count):
    _, chunks, half, _ = attended.shape
    width = w_out.shape[1]
    depth = gx_count // 2
    keep = depth // 2
    vmem = pl.BlockSpec(memory_space=pltpu.VMEM)
    dma = pltpu.SemaphoreType.DMA
    return pl.pallas_call(
        functools.partial(output_kernel, gx_count),
        out_shape=jax.ShapeDtypeStruct((keep, 2, 2 * half, width), jnp.bfloat16),
        in_specs=[vmem, pl.BlockSpec(memory_space=pl.ANY)],
        out_specs=vmem,
        scratch_shapes=[
            pltpu.VMEM((chunks, CHUNK, width), jnp.bfloat16),
            pltpu.VMEM((chunks, 2, depth, 2, half, CHUNK), jnp.bfloat16),
            pltpu.VMEM((2, depth, 2 * half, width), jnp.float32),
            pltpu.VMEM((2, keep, 2 * half, width), jnp.float32),
            dma((chunks,)),
            dma((2,)),
            dma((chunks, depth)),
            dma((chunks, depth)),
            dma((chunks, depth)),
            dma((chunks, depth)),
            dma((2,)),
        ],
        compiler_params=pltpu.CompilerParams(
            collective_id=2, has_side_effects=True, vmem_limit_bytes=56 * 1024 * 1024
        ),
    )(attended, w_out)


def attend_kernel(steps, lengths_ref, q_ref, kn_ref, vn_ref, k_ref, v_ref, out_ref):
    live = lengths_ref[pl.program_id(0)]
    total = k_ref.shape[1]
    block = total // 4
    for count in range(1, 5):

        @pl.when((live > (count - 1) * block) & (live <= count * block))
        def _():
            attend_slots(
                steps, count * block, live, q_ref, kn_ref, vn_ref, k_ref, v_ref, out_ref
            )


def attend_slots(steps, slots, live, q_ref, kn_ref, vn_ref, k_ref, v_ref, out_ref):
    kv_heads, queries, head_dim = q_ref.shape[1:]
    inverse = 1.0 / math.sqrt(head_dim)
    mask = lax.broadcasted_iota(jnp.int32, (queries, slots), 1) < live
    step = lax.broadcasted_iota(jnp.int32, (queries, 1), 0) // (queries // steps)
    for g in range(kv_heads):
        cols = slice(g * head_dim, (g + 1) * head_dim)
        q = q_ref[0, g]
        scores = (
            lax.dot_general(
                q, k_ref[0, :slots, cols], (((1,), (1,)), ((), ())), preferred_element_type=jnp.float32
            )
            * inverse
        )
        scores = jnp.where(mask, scores, -jnp.inf)
        wide = q.astype(jnp.float32)
        highest = jnp.max(scores, axis=1, keepdims=True)
        fresh = []
        for s in range(steps):
            one = (
                jnp.sum(wide * kn_ref[0, s : s + 1, cols].astype(jnp.float32), axis=1, keepdims=True)
                * inverse
            )
            one = jnp.where(step >= s, one, -jnp.inf)
            highest = jnp.maximum(highest, one)
            fresh.append(one)
        exp_cache = jnp.exp(scores - highest)
        denominator = jnp.sum(exp_cache, axis=1, keepdims=True)
        exp_new = [jnp.exp(one - highest) for one in fresh]
        for one in exp_new:
            denominator = denominator + one
        scale = 1.0 / denominator
        weights = (exp_cache * scale).astype(jnp.bfloat16)
        result = jnp.dot(weights, v_ref[0, :slots, cols], preferred_element_type=jnp.float32)
        for s in range(steps):
            weight = (exp_new[s] * scale).astype(jnp.bfloat16).astype(jnp.float32)
            result = result + weight * vn_ref[0, s : s + 1, cols].astype(jnp.float32)
        out_ref[0, g] = result.astype(jnp.bfloat16)


def attend(lengths, queries, keys_new, values_new, keys, values):
    rows, kv_heads, count, head_dim = queries.shape
    steps = keys_new.shape[1]
    slots, width = keys.shape[1:]
    return pl.pallas_call(
        functools.partial(attend_kernel, steps),
        out_shape=jax.ShapeDtypeStruct(queries.shape, jnp.bfloat16),
        grid_spec=pltpu.PrefetchScalarGridSpec(
            num_scalar_prefetch=1,
            grid=(rows,),
            in_specs=[
                pl.BlockSpec((1, kv_heads, count, head_dim), lambda r, _: (r, 0, 0, 0)),
                pl.BlockSpec((1, steps, width), lambda r, _: (r, 0, 0)),
                pl.BlockSpec((1, steps, width), lambda r, _: (r, 0, 0)),
                pl.BlockSpec((1, slots, width), lambda r, _: (r, 0, 0)),
                pl.BlockSpec((1, slots, width), lambda r, _: (r, 0, 0)),
            ],
            out_specs=pl.BlockSpec((1, kv_heads, count, head_dim), lambda r, _: (r, 0, 0, 0)),
        ),
        compiler_params=pltpu.CompilerParams(vmem_limit_bytes=56 * 1024 * 1024),
    )(lengths, queries, keys_new, values_new, keys, values)


def rotary_embed(inputs, token_positions):
    half_dim = inputs.shape[-1] // 2
    frequency = rope_base ** (-jnp.arange(half_dim, dtype=jnp.float32) / half_dim)
    angles = token_positions.astype(jnp.float32)[..., None, None] * frequency
    cosine = jnp.cos(angles)
    sine_part = jnp.sin(angles)
    lower_half = inputs[..., :half_dim]
    upper_half = inputs[..., half_dim:]
    return jnp.concatenate(
        [
            lower_half * cosine - upper_half * sine_part,
            upper_half * cosine + lower_half * sine_part,
        ],
        axis=-1,
    )


def local(
    hidden,
    norm_gain,
    w_query,
    key_weight,
    value_weight,
    w_out,
    stored_rotated_keys,
    stored_value_rows,
    lengths,
):
    gx_count = lax.axis_size("gx")
    gy_count = lax.axis_size("gy")
    steps, width = hidden.shape[1:]
    head_dim = HEAD_SIZE
    local_rows = lengths.shape[0]
    key_width = key_weight.shape[1]
    kv_heads = key_width * gy_count // head_dim
    mixed = project(
        hidden.reshape(-1, width),
        norm_gain.reshape(1, width),
        w_query,
        key_weight,
        value_weight,
        gx_count,
    )
    query_part = mixed[:, :-1]
    chunks = query_part.shape[1]
    per_chunk = CHUNK // head_dim
    queries = query_part.reshape(gy_count, chunks, local_rows, steps, per_chunk, head_dim)
    queries = queries.transpose(2, 3, 0, 1, 4, 5).reshape(local_rows, steps, -1, head_dim)
    fresh = mixed[:, -1].reshape(gy_count, local_rows, steps, 2, key_width).transpose(1, 2, 3, 0, 4)
    keys_new = fresh[:, :, 0].reshape(local_rows, steps, -1, head_dim)
    values_new = fresh[:, :, 1].reshape(local_rows, steps, -1)
    token_positions = lengths[:, None] + jnp.arange(steps)
    queries = rotary_embed(queries.astype(jnp.float32), token_positions).astype(jnp.bfloat16)
    keys_new = rotary_embed(keys_new.astype(jnp.float32), token_positions).astype(jnp.bfloat16)
    per_group = queries.shape[2] // kv_heads
    queries = queries.reshape(local_rows, steps, kv_heads, per_group, head_dim)
    queries = queries.transpose(0, 2, 1, 3, 4).reshape(
        local_rows, kv_heads, steps * per_group, head_dim
    )
    attended = attend(
        lengths,
        queries,
        keys_new.reshape(local_rows, steps, -1),
        values_new,
        stored_rotated_keys,
        stored_value_rows,
    )
    attended = attended.reshape(local_rows, gy_count, -1, steps, per_group // per_chunk, CHUNK)
    attended = attended.transpose(1, 2, 4, 0, 3, 5).reshape(
        gy_count, chunks, local_rows * steps, CHUNK
    )
    result = output(attended, w_out, gx_count)
    return result.reshape(-1, steps, width)


def solution(mesh):
    return jax.shard_map(
        local,
        mesh=mesh,
        in_specs=(
            P(("groups", "gy"), None, "gx"),
            P("gx"),
            P("gx", "gy"),
            P("gx", "gy"),
            P("gx", "gy"),
            P("gy", "gx"),
            P(("groups", "gx", "gy"), None, None),
            P(("groups", "gx", "gy"), None, None),
            P(("groups", "gx", "gy")),
        ),
        out_specs=P(("groups", "gy"), None, "gx"),
        check_vma=False,
    )
```

```python
import functools
import math

import jax
import jax.numpy as jnp
from jax import lax
from jax.experimental import pallas as pl
from jax.experimental.pallas import tpu as pltpu
from jax.sharding import PartitionSpec as P

HEAD_SIZE = 128
CHUNK = 512
WIRE = jnp.int16
SMALL = 2.0**-20
CODES = 32767.0 / math.log(2.0**34.5)
epsilon = 1e-05
rope_base = 500000.0


def encode(values):
    size = jnp.log(1.0 + jnp.abs(values) * (1.0 / SMALL)) * CODES + 0.5
    return jnp.where(values < 0, -size, size).astype(jnp.int32).astype(WIRE)


def decode(codes):
    wide = codes.astype(jnp.int32).astype(jnp.float32)
    size = jnp.exp(jnp.abs(wide) * (1.0 / CODES)) * SMALL - SMALL
    return jnp.where(wide < 0, -size, size)


def remote(src, dst, send, recv, device):
    return pltpu.make_async_remote_copy(
        src_ref=src,
        dst_ref=dst,
        send_sem=send,
        recv_sem=recv,
        device_id=device,
        device_id_type=pl.DeviceIdType.MESH,
    )


def position(gx_count):
    gx = lax.axis_index("gx")
    core = lax.axis_index("gy")
    depth = gx_count // 2
    far, near = gx // 2, lax.rem(gx, 2)
    sibling = {"gy": 1 - core}
    pair = {"gx": far * 2 + (1 - near)}

    def line(d):
        return {"gx": lax.rem(far + d, depth) * 2 + near}

    return core, far, near, sibling, pair, line


def greet(sibling, pair, line, depth):
    barrier = pltpu.get_barrier_semaphore()
    devices = [sibling, pair] + [line(d) for d in range(1, depth)]
    for device in devices:
        pl.semaphore_signal(
            barrier, inc=1, device_id=device, device_id_type=pl.DeviceIdType.MESH
        )
    pl.semaphore_wait(barrier, len(devices))


def project_kernel(
    gx_count,
    rows_block,
    x_ref,
    gain_ref,
    wq_ref,
    kw_ref,
    vw_ref,
    out_ref,
    wbuf,
    xs,
    sums,
    mine,
    mid,
    pair_sums,
    line_sums,
    normed,
    own,
    s1,
    r1,
    s2,
    r2,
    fin,
    fin_in,
    wsem,
    xsem,
    psem,
    lsem,
    s1s,
    s1r,
    s2s,
    s2r,
    fsem,
):
    depth = gx_count // 2
    chunks, width, _ = wbuf.shape
    half_rows = xs.shape[1]
    rows = 2 * half_rows
    key_width = kw_ref.shape[1]
    core, far, near, sibling, pair, line = position(gx_count)

    def load_query(c):
        return pltpu.make_async_copy(
            wq_ref.at[:, pl.ds(pl.multiple_of(c * CHUNK, CHUNK), CHUNK)],
            wbuf.at[c],
            wsem.at[c],
        )

    load_key = pltpu.make_async_copy(
        kw_ref, wbuf.at[chunks - 1, :, pl.ds(0, key_width)], wsem.at[chunks - 1]
    )
    load_value = pltpu.make_async_copy(
        vw_ref, wbuf.at[chunks - 1, :, pl.ds(key_width, key_width)], wsem.at[chunks]
    )

    @pl.loop(0, chunks - 1)
    def _(c):
        load_query(c).start()

    load_key.start()
    load_value.start()
    greet(sibling, pair, line, depth)

    send_x = remote(x_ref, xs.at[core], xsem.at[0], xsem.at[1], sibling)
    send_x.start()
    xs[core] = x_ref[...]

    def row_sums(g):
        wide = xs[g].astype(jnp.float32)
        column = jnp.sum(wide * wide, axis=1, keepdims=True)
        sums[g] = jnp.transpose(jnp.broadcast_to(column, (half_rows, 128)))[0:8, :]

    row_sums(core)
    send_x.wait()
    row_sums(1 - core)
    mine[...] = jnp.concatenate([sums[0], sums[1]], axis=1)
    swap = remote(mine, pair_sums, psem.at[0], psem.at[1], pair)
    swap.start()
    swap.wait()
    mid[...] = mine[...] + pair_sums[...]
    line_copies = [
        remote(mid, line_sums.at[d], lsem.at[0, d], lsem.at[1, d], line(d))
        for d in range(1, depth)
    ]
    for copy in line_copies:
        copy.start()
    for copy in line_copies:
        copy.wait()
    total = mid[...]
    for d in range(1, depth):
        total = total + line_sums[d]
    factor_row = lax.rsqrt(total * (1.0 / (width * gx_count)) + epsilon)
    factor = jnp.transpose(jnp.broadcast_to(factor_row[0:1, :], (128, rows)))[:, 0:1]
    gain = gain_ref[...].astype(jnp.float32)
    blocks_half = half_rows // rows_block
    for b in range(2 * blocks_half):
        start = (b % blocks_half) * rows_block
        wide = xs[b // blocks_half, start : start + rows_block, :].astype(jnp.float32)
        scaled = wide * factor[b * rows_block : (b + 1) * rows_block, :] * gain
        normed[(b % 2) * depth + b // 2] = scaled.astype(jnp.bfloat16)

    def first(c):
        return remote(s1.at[c], r1.at[c], s1s.at[c], s1r.at[c], pair)

    def second(c, d):
        return remote(
            s2.at[c, lax.rem(far + d, depth)], r2.at[c, d], s2s.at[c, d], s2r.at[c, d], line(d)
        )

    lag = 2

    @pl.loop(0, chunks + lag)
    def _(c):
        @pl.when(c < chunks)
        def _():
            @pl.when(c < chunks - 1)
            def _():
                load_query(c).wait()

            @pl.when(c == chunks - 1)
            def _():
                load_key.wait()
                load_value.wait()

            part = jnp.dot(
                normed[...].reshape(rows, width), wbuf[c], preferred_element_type=jnp.float32
            ).reshape(2, depth, rows_block, CHUNK)

            @pl.when(near == 0)
            def _():
                own[c] = part[0]
                s1[c] = encode(part[1])

            @pl.when(near == 1)
            def _():
                own[c] = part[1]
                s1[c] = encode(part[0])

            first(c).start()

        @pl.when(c >= lag)
        def _():
            cc = c - lag
            first(cc).wait_recv()
            both = own[cc] + decode(r1[cc])
            own[cc] = both
            s2[cc] = encode(both)
            for d in range(1, depth):
                second(cc, d).start()

    @pl.loop(0, chunks)
    def _(c):
        summed = own[c, far]
        for d in range(1, depth):
            second(c, d).wait_recv()
            summed = summed + decode(r2[c, d])
        rounded = summed.astype(jnp.bfloat16)
        for g in range(2):
            fin[g, c] = rounded[g * (rows_block // 2) : (g + 1) * (rows_block // 2), :]

    last = remote(fin.at[1 - core], fin_in, fsem.at[0], fsem.at[1], sibling)
    last.start()
    out_ref[core] = fin[core]

    @pl.loop(0, chunks)
    def _(c):
        first(c).wait_send()
        for d in range(1, depth):
            second(c, d).wait_send()

    last.wait()
    out_ref[1 - core] = fin_in[...]


def project(x, gain, w_query, key_weight, value_weight, gx_count):
    half_rows, width = x.shape
    rows = 2 * half_rows
    rows_block = rows // gx_count
    depth = gx_count // 2
    chunks = w_query.shape[1] // CHUNK + 1
    out_rows = rows_block // 2
    vmem = pl.BlockSpec(memory_space=pltpu.VMEM)
    hbm = pl.BlockSpec(memory_space=pl.ANY)
    dma = pltpu.SemaphoreType.DMA
    return pl.pallas_call(
        functools.partial(project_kernel, gx_count, rows_block),
        out_shape=jax.ShapeDtypeStruct((2, chunks, out_rows, CHUNK), jnp.bfloat16),
        in_specs=[vmem, vmem, hbm, hbm, hbm],
        out_specs=vmem,
        scratch_shapes=[
            pltpu.VMEM((chunks, width, CHUNK), jnp.bfloat16),
            pltpu.VMEM((2, half_rows, width), jnp.bfloat16),
            pltpu.VMEM((2, 8, half_rows), jnp.float32),
            pltpu.VMEM((8, rows), jnp.float32),
            pltpu.VMEM((8, rows), jnp.float32),
            pltpu.VMEM((8, rows), jnp.float32),
            pltpu.VMEM((depth, 8, rows), jnp.float32),
            pltpu.VMEM((2 * depth, rows_block, width), jnp.bfloat16),
            pltpu.VMEM((chunks, depth, rows_block, CHUNK), jnp.float32),
            pltpu.VMEM((chunks, depth, rows_block, CHUNK), WIRE),
            pltpu.VMEM((chunks, depth, rows_block, CHUNK), WIRE),
            pltpu.VMEM((chunks, depth, rows_block, CHUNK), WIRE),
            pltpu.VMEM((chunks, depth, rows_block, CHUNK), WIRE),
            pltpu.VMEM((2, chunks, out_rows, CHUNK), jnp.bfloat16),
            pltpu.VMEM((chunks, out_rows, CHUNK), jnp.bfloat16),
            dma((chunks + 1,)),
            dma((2,)),
            dma((2,)),
            dma((2, depth)),
            dma((chunks,)),
            dma((chunks,)),
            dma((chunks, depth)),
            dma((chunks, depth)),
            dma((2,)),
        ],
        compiler_params=pltpu.CompilerParams(
            collective_id=1, has_side_effects=True, vmem_limit_bytes=56 * 1024 * 1024
        ),
    )(x, gain, w_query, key_weight, value_weight)


def output_kernel(
    gx_count,
    att_ref,
    w_ref,
    out_ref,
    wbuf,
    full,
    acc,
    acc_in,
    wsem,
    gsem,
    zs,
    zr,
    ys,
    yr,
    fsem,
):
    depth = gx_count // 2
    chunks = wbuf.shape[0]
    width = wbuf.shape[2]
    _, _, _, _, half, _ = full.shape
    rows = 2 * depth * 2 * half
    core, far, near, sibling, pair, line = position(gx_count)

    def load(c):
        return pltpu.make_async_copy(
            w_ref.at[pl.ds(pl.multiple_of(c * CHUNK, CHUNK), CHUNK), :], wbuf.at[c], wsem.at[c]
        )

    @pl.loop(0, chunks)
    def _(c):
        load(c).start()

    greet(sibling, pair, line, depth)
    give = remote(
        att_ref.at[1 - core],
        full.at[:, near, far, core],
        gsem.at[0],
        gsem.at[1],
        sibling,
    )
    give.start()

    @pl.loop(0, chunks)
    def _(c):
        full[c, near, far, core] = att_ref[core, c]

    acc[...] = jnp.zeros_like(acc)
    give.wait()

    def along(c, d):
        block = full.at[c, near, far]
        return remote(block, block, zs.at[c, d], zr.at[c, d], line(d))

    def across(c, d):
        block = full.at[c, near, lax.rem(far + depth - d, depth)]
        return remote(block, block, ys.at[c, d], yr.at[c, d], pair)

    ahead = 2
    lag = ahead + 1

    @pl.loop(0, chunks + lag)
    def _(c):
        @pl.when(c < chunks)
        def _():
            for d in range(depth - 1, 0, -1):
                along(c, d).start()
            across(c, 0).start()

        @pl.when((c >= ahead) & (c < chunks + ahead))
        def _():
            for d in range(1, depth):
                along(c - ahead, d).wait_recv()
                across(c - ahead, d).start()

        @pl.when(c >= lag)
        def _():
            cc = c - lag
            for d in range(depth):
                across(cc, d).wait_recv()
            load(cc).wait()
            acc[...] += jnp.dot(
                full[cc].reshape(rows, CHUNK), wbuf[cc], preferred_element_type=jnp.float32
            ).reshape(2, depth, 2 * half, width)

    keep = depth // 2
    last = remote(
        acc.at[:, pl.ds((1 - core) * keep, keep)], acc_in, fsem.at[0], fsem.at[1], sibling
    )
    last.start()

    @pl.loop(0, chunks)
    def _(c):
        across(c, 0).wait_send()
        for d in range(1, depth):
            along(c, d).wait_send()
            across(c, d).wait_send()

    last.wait()
    for z in range(keep):
        for y in range(2):
            out_ref[z, y] = (acc[y, core * keep + z] + acc_in[y, z]).astype(out_ref.dtype)


def output(attended, w_out, gx_count):
    _, chunks, half, _ = attended.shape
    width = w_out.shape[1]
    depth = gx_count // 2
    keep = depth // 2
    vmem = pl.BlockSpec(memory_space=pltpu.VMEM)
    dma = pltpu.SemaphoreType.DMA
    return pl.pallas_call(
        functools.partial(output_kernel, gx_count),
        out_shape=jax.ShapeDtypeStruct((keep, 2, 2 * half, width), jnp.bfloat16),
        in_specs=[vmem, pl.BlockSpec(memory_space=pl.ANY)],
        out_specs=vmem,
        scratch_shapes=[
            pltpu.VMEM((chunks, CHUNK, width), jnp.bfloat16),
            pltpu.VMEM((chunks, 2, depth, 2, half, CHUNK), jnp.bfloat16),
            pltpu.VMEM((2, depth, 2 * half, width), jnp.float32),
            pltpu.VMEM((2, keep, 2 * half, width), jnp.float32),
            dma((chunks,)),
            dma((2,)),
            dma((chunks, depth)),
            dma((chunks, depth)),
            dma((chunks, depth)),
            dma((chunks, depth)),
            dma((2,)),
        ],
        compiler_params=pltpu.CompilerParams(
            collective_id=2, has_side_effects=True, vmem_limit_bytes=56 * 1024 * 1024
        ),
    )(attended, w_out)


def attend_kernel(steps, lengths_ref, q_ref, kn_ref, vn_ref, k_ref, v_ref, out_ref):
    live = lengths_ref[pl.program_id(0)]
    total = k_ref.shape[1]
    block = total // 4
    for count in range(1, 5):

        @pl.when((live > (count - 1) * block) & (live <= count * block))
        def _():
            attend_slots(
                steps, count * block, live, q_ref, kn_ref, vn_ref, k_ref, v_ref, out_ref
            )


def attend_slots(steps, slots, live, q_ref, kn_ref, vn_ref, k_ref, v_ref, out_ref):
    kv_heads, queries, head_dim = q_ref.shape[1:]
    inverse = 1.0 / math.sqrt(head_dim)
    mask = lax.broadcasted_iota(jnp.int32, (queries, slots), 1) < live
    step = lax.broadcasted_iota(jnp.int32, (queries, 1), 0) // (queries // steps)
    heads = [slice(g * head_dim, (g + 1) * head_dim) for g in range(kv_heads)]
    mask = jnp.concatenate([mask] * kv_heads, axis=0)
    scores = [
        lax.dot_general(
            q_ref[0, g],
            k_ref[0, :slots, cols],
            (((1,), (1,)), ((), ())),
            preferred_element_type=jnp.float32,
        )
        for g, cols in enumerate(heads)
    ]
    scores = jnp.where(mask, jnp.concatenate(scores, axis=0) * inverse, -jnp.inf)
    highest = jnp.max(scores, axis=1, keepdims=True)
    fresh = []
    for s in range(steps):
        one = [
            jnp.sum(
                q_ref[0, g].astype(jnp.float32) * kn_ref[0, s : s + 1, cols].astype(jnp.float32),
                axis=1,
                keepdims=True,
            )
            * inverse
            for g, cols in enumerate(heads)
        ]
        one = jnp.concatenate([jnp.where(step >= s, part, -jnp.inf) for part in one], axis=0)
        highest = jnp.maximum(highest, one)
        fresh.append(one)
    exp_cache = jnp.exp(scores - highest)
    denominator = jnp.sum(exp_cache, axis=1, keepdims=True)
    exp_new = [jnp.exp(one - highest) for one in fresh]
    for one in exp_new:
        denominator = denominator + one
    scale = 1.0 / denominator
    weights = (exp_cache * scale).astype(jnp.bfloat16)
    new_weights = [(one * scale).astype(jnp.bfloat16).astype(jnp.float32) for one in exp_new]
    for g, cols in enumerate(heads):
        rows = slice(g * queries, (g + 1) * queries)
        result = jnp.dot(
            weights[rows, :], v_ref[0, :slots, cols], preferred_element_type=jnp.float32
        )
        for s in range(steps):
            result = result + new_weights[s][rows, :] * vn_ref[0, s : s + 1, cols].astype(
                jnp.float32
            )
        out_ref[0, g] = result.astype(jnp.bfloat16)


def attend(lengths, queries, keys_new, values_new, keys, values):
    rows, kv_heads, count, head_dim = queries.shape
    steps = keys_new.shape[1]
    slots, width = keys.shape[1:]
    return pl.pallas_call(
        functools.partial(attend_kernel, steps),
        out_shape=jax.ShapeDtypeStruct(queries.shape, jnp.bfloat16),
        grid_spec=pltpu.PrefetchScalarGridSpec(
            num_scalar_prefetch=1,
            grid=(rows,),
            in_specs=[
                pl.BlockSpec((1, kv_heads, count, head_dim), lambda r, _: (r, 0, 0, 0)),
                pl.BlockSpec((1, steps, width), lambda r, _: (r, 0, 0)),
                pl.BlockSpec((1, steps, width), lambda r, _: (r, 0, 0)),
                pl.BlockSpec((1, slots, width), lambda r, _: (r, 0, 0)),
                pl.BlockSpec((1, slots, width), lambda r, _: (r, 0, 0)),
            ],
            out_specs=pl.BlockSpec((1, kv_heads, count, head_dim), lambda r, _: (r, 0, 0, 0)),
        ),
        compiler_params=pltpu.CompilerParams(vmem_limit_bytes=56 * 1024 * 1024),
    )(lengths, queries, keys_new, values_new, keys, values)


def rotary_embed(inputs, token_positions):
    half_dim = inputs.shape[-1] // 2
    frequency = rope_base ** (-jnp.arange(half_dim, dtype=jnp.float32) / half_dim)
    angles = token_positions.astype(jnp.float32)[..., None, None] * frequency
    cosine = jnp.cos(angles)
    sine_part = jnp.sin(angles)
    lower_half = inputs[..., :half_dim]
    upper_half = inputs[..., half_dim:]
    return jnp.concatenate(
        [
            lower_half * cosine - upper_half * sine_part,
            upper_half * cosine + lower_half * sine_part,
        ],
        axis=-1,
    )


def local(
    hidden,
    norm_gain,
    w_query,
    key_weight,
    value_weight,
    w_out,
    stored_rotated_keys,
    stored_value_rows,
    lengths,
):
    gx_count = lax.axis_size("gx")
    gy_count = lax.axis_size("gy")
    steps, width = hidden.shape[1:]
    head_dim = HEAD_SIZE
    local_rows = lengths.shape[0]
    key_width = key_weight.shape[1]
    kv_heads = key_width * gy_count // head_dim
    mixed = project(
        hidden.reshape(-1, width),
        norm_gain.reshape(1, width),
        w_query,
        key_weight,
        value_weight,
        gx_count,
    )
    query_part = mixed[:, :-1]
    chunks = query_part.shape[1]
    per_chunk = CHUNK // head_dim
    queries = query_part.reshape(gy_count, chunks, local_rows, steps, per_chunk, head_dim)
    queries = queries.transpose(2, 3, 0, 1, 4, 5).reshape(local_rows, steps, -1, head_dim)
    fresh = mixed[:, -1].reshape(gy_count, local_rows, steps, 2, key_width).transpose(1, 2, 3, 0, 4)
    keys_new = fresh[:, :, 0].reshape(local_rows, steps, -1, head_dim)
    values_new = fresh[:, :, 1].reshape(local_rows, steps, -1)
    token_positions = lengths[:, None] + jnp.arange(steps)
    queries = rotary_embed(queries.astype(jnp.float32), token_positions).astype(jnp.bfloat16)
    keys_new = rotary_embed(keys_new.astype(jnp.float32), token_positions).astype(jnp.bfloat16)
    per_group = queries.shape[2] // kv_heads
    queries = queries.reshape(local_rows, steps, kv_heads, per_group, head_dim)
    queries = queries.transpose(0, 2, 1, 3, 4).reshape(
        local_rows, kv_heads, steps * per_group, head_dim
    )
    attended = attend(
        lengths,
        queries,
        keys_new.reshape(local_rows, steps, -1),
        values_new,
        stored_rotated_keys,
        stored_value_rows,
    )
    attended = attended.reshape(local_rows, gy_count, -1, steps, per_group // per_chunk, CHUNK)
    attended = attended.transpose(1, 2, 4, 0, 3, 5).reshape(
        gy_count, chunks, local_rows * steps, CHUNK
    )
    result = output(attended, w_out, gx_count)
    return result.reshape(-1, steps, width)


def solution(mesh):
    return jax.shard_map(
        local,
        mesh=mesh,
        in_specs=(
            P(("groups", "gy"), None, "gx"),
            P("gx"),
            P("gx", "gy"),
            P("gx", "gy"),
            P("gx", "gy"),
            P("gy", "gx"),
            P(("groups", "gx", "gy"), None, None),
            P(("groups", "gx", "gy"), None, None),
            P(("groups", "gx", "gy")),
        ),
        out_specs=P(("groups", "gy"), None, "gx"),
        check_vma=False,
    )
```

```python
import functools
import math

import jax
import jax.numpy as jnp
from jax import lax
from jax.experimental import pallas as pl
from jax.experimental.pallas import tpu as pltpu
from jax.sharding import PartitionSpec as P

HEAD_SIZE = 128
CHUNK = 512
OUT_CHUNK = 1024
WIRE = jnp.int16
SMALL = 2.0**-20
CODES = 32767.0 / math.log(2.0**34.5)
epsilon = 1e-05
rope_base = 500000.0


def encode(values):
    size = jnp.log(1.0 + jnp.abs(values) * (1.0 / SMALL)) * CODES + 0.5
    return jnp.where(values < 0, -size, size).astype(jnp.int32).astype(WIRE)


def decode(codes):
    wide = codes.astype(jnp.int32).astype(jnp.float32)
    size = jnp.exp(jnp.abs(wide) * (1.0 / CODES)) * SMALL - SMALL
    return jnp.where(wide < 0, -size, size)


def remote(src, dst, send, recv, device):
    return pltpu.make_async_remote_copy(
        src_ref=src,
        dst_ref=dst,
        send_sem=send,
        recv_sem=recv,
        device_id=device,
        device_id_type=pl.DeviceIdType.MESH,
    )


def position(gx_count):
    gx = lax.axis_index("gx")
    core = lax.axis_index("gy")
    depth = gx_count // 2
    far, near = gx // 2, lax.rem(gx, 2)
    sibling = {"gy": 1 - core}
    pair = {"gx": far * 2 + (1 - near)}

    def line(d):
        return {"gx": lax.rem(far + d, depth) * 2 + near}

    return core, far, near, sibling, pair, line


def greet(sibling, pair, line, depth):
    barrier = pltpu.get_barrier_semaphore()
    devices = [sibling, pair] + [line(d) for d in range(1, depth)]
    for device in devices:
        pl.semaphore_signal(
            barrier, inc=1, device_id=device, device_id_type=pl.DeviceIdType.MESH
        )
    pl.semaphore_wait(barrier, len(devices))


def project_kernel(
    gx_count,
    rows_block,
    x_ref,
    gain_ref,
    wq_ref,
    kw_ref,
    vw_ref,
    out_ref,
    wbuf,
    xs,
    sums,
    mine,
    mid,
    pair_sums,
    line_sums,
    normed,
    own,
    s1,
    r1,
    s2,
    r2,
    fin,
    fin_in,
    wsem,
    xsem,
    psem,
    lsem,
    s1s,
    s1r,
    s2s,
    s2r,
    fsem,
):
    depth = gx_count // 2
    chunks, width, _ = wbuf.shape
    half_rows = xs.shape[1]
    rows = 2 * half_rows
    key_width = kw_ref.shape[1]
    core, far, near, sibling, pair, line = position(gx_count)

    def load_query(c):
        return pltpu.make_async_copy(
            wq_ref.at[:, pl.ds(pl.multiple_of(c * CHUNK, CHUNK), CHUNK)],
            wbuf.at[c],
            wsem.at[c],
        )

    load_key = pltpu.make_async_copy(
        kw_ref, wbuf.at[chunks - 1, :, pl.ds(0, key_width)], wsem.at[chunks - 1]
    )
    load_value = pltpu.make_async_copy(
        vw_ref, wbuf.at[chunks - 1, :, pl.ds(key_width, key_width)], wsem.at[chunks]
    )

    @pl.loop(0, chunks - 1)
    def _(c):
        load_query(c).start()

    load_key.start()
    load_value.start()
    greet(sibling, pair, line, depth)

    send_x = remote(x_ref, xs.at[core], xsem.at[0], xsem.at[1], sibling)
    send_x.start()
    xs[core] = x_ref[...]

    def row_sums(g):
        wide = xs[g].astype(jnp.float32)
        column = jnp.sum(wide * wide, axis=1, keepdims=True)
        sums[g] = jnp.transpose(jnp.broadcast_to(column, (half_rows, 128)))[0:8, :]

    row_sums(core)
    send_x.wait()
    row_sums(1 - core)
    mine[...] = jnp.concatenate([sums[0], sums[1]], axis=1)
    swap = remote(mine, pair_sums, psem.at[0], psem.at[1], pair)
    swap.start()
    swap.wait()
    mid[...] = mine[...] + pair_sums[...]
    line_copies = [
        remote(mid, line_sums.at[d], lsem.at[0, d], lsem.at[1, d], line(d))
        for d in range(1, depth)
    ]
    for copy in line_copies:
        copy.start()
    for copy in line_copies:
        copy.wait()
    total = mid[...]
    for d in range(1, depth):
        total = total + line_sums[d]
    factor_row = lax.rsqrt(total * (1.0 / (width * gx_count)) + epsilon)
    factor = jnp.transpose(jnp.broadcast_to(factor_row[0:1, :], (128, rows)))[:, 0:1]
    gain = gain_ref[...].astype(jnp.float32)
    blocks_half = half_rows // rows_block
    for b in range(2 * blocks_half):
        start = (b % blocks_half) * rows_block
        wide = xs[b // blocks_half, start : start + rows_block, :].astype(jnp.float32)
        scaled = wide * factor[b * rows_block : (b + 1) * rows_block, :] * gain
        normed[(b % 2) * depth + b // 2] = scaled.astype(jnp.bfloat16)

    def first(c):
        return remote(s1.at[c], r1.at[c], s1s.at[c], s1r.at[c], pair)

    def second(c, d):
        return remote(
            s2.at[c, lax.rem(far + d, depth)], r2.at[c, d], s2s.at[c, d], s2r.at[c, d], line(d)
        )

    lag = 2

    @pl.loop(0, chunks + lag)
    def _(c):
        @pl.when(c < chunks)
        def _():
            @pl.when(c < chunks - 1)
            def _():
                load_query(c).wait()

            @pl.when(c == chunks - 1)
            def _():
                load_key.wait()
                load_value.wait()

            part = jnp.dot(
                normed[...].reshape(rows, width), wbuf[c], preferred_element_type=jnp.float32
            ).reshape(2, depth, rows_block, CHUNK)

            @pl.when(near == 0)
            def _():
                own[c] = part[0]
                s1[c] = encode(part[1])

            @pl.when(near == 1)
            def _():
                own[c] = part[1]
                s1[c] = encode(part[0])

            first(c).start()

        @pl.when(c >= lag)
        def _():
            cc = c - lag
            first(cc).wait_recv()
            both = own[cc] + decode(r1[cc])
            own[cc] = both
            s2[cc] = encode(both)
            for d in range(1, depth):
                second(cc, d).start()

    @pl.loop(0, chunks)
    def _(c):
        summed = own[c, far]
        for d in range(1, depth):
            second(c, d).wait_recv()
            summed = summed + decode(r2[c, d])
        rounded = summed.astype(jnp.bfloat16)
        for g in range(2):
            fin[g, c] = rounded[g * (rows_block // 2) : (g + 1) * (rows_block // 2), :]

    last = remote(fin.at[1 - core], fin_in, fsem.at[0], fsem.at[1], sibling)
    last.start()
    out_ref[core] = fin[core]

    @pl.loop(0, chunks)
    def _(c):
        first(c).wait_send()
        for d in range(1, depth):
            second(c, d).wait_send()

    last.wait()
    out_ref[1 - core] = fin_in[...]


def project(x, gain, w_query, key_weight, value_weight, gx_count):
    half_rows, width = x.shape
    rows = 2 * half_rows
    rows_block = rows // gx_count
    depth = gx_count // 2
    chunks = w_query.shape[1] // CHUNK + 1
    out_rows = rows_block // 2
    vmem = pl.BlockSpec(memory_space=pltpu.VMEM)
    hbm = pl.BlockSpec(memory_space=pl.ANY)
    dma = pltpu.SemaphoreType.DMA
    return pl.pallas_call(
        functools.partial(project_kernel, gx_count, rows_block),
        out_shape=jax.ShapeDtypeStruct((2, chunks, out_rows, CHUNK), jnp.bfloat16),
        in_specs=[vmem, vmem, hbm, hbm, hbm],
        out_specs=vmem,
        scratch_shapes=[
            pltpu.VMEM((chunks, width, CHUNK), jnp.bfloat16),
            pltpu.VMEM((2, half_rows, width), jnp.bfloat16),
            pltpu.VMEM((2, 8, half_rows), jnp.float32),
            pltpu.VMEM((8, rows), jnp.float32),
            pltpu.VMEM((8, rows), jnp.float32),
            pltpu.VMEM((8, rows), jnp.float32),
            pltpu.VMEM((depth, 8, rows), jnp.float32),
            pltpu.VMEM((2 * depth, rows_block, width), jnp.bfloat16),
            pltpu.VMEM((chunks, depth, rows_block, CHUNK), jnp.float32),
            pltpu.VMEM((chunks, depth, rows_block, CHUNK), WIRE),
            pltpu.VMEM((chunks, depth, rows_block, CHUNK), WIRE),
            pltpu.VMEM((chunks, depth, rows_block, CHUNK), WIRE),
            pltpu.VMEM((chunks, depth, rows_block, CHUNK), WIRE),
            pltpu.VMEM((2, chunks, out_rows, CHUNK), jnp.bfloat16),
            pltpu.VMEM((chunks, out_rows, CHUNK), jnp.bfloat16),
            dma((chunks + 1,)),
            dma((2,)),
            dma((2,)),
            dma((2, depth)),
            dma((chunks,)),
            dma((chunks,)),
            dma((chunks, depth)),
            dma((chunks, depth)),
            dma((2,)),
        ],
        compiler_params=pltpu.CompilerParams(
            collective_id=1, has_side_effects=True, vmem_limit_bytes=56 * 1024 * 1024
        ),
    )(x, gain, w_query, key_weight, value_weight)


def output_kernel(
    gx_count,
    att_ref,
    w_ref,
    out_ref,
    wbuf,
    full,
    acc,
    acc_in,
    wsem,
    gsem,
    zs,
    zr,
    ys,
    yr,
    fsem,
):
    depth = gx_count // 2
    chunks = wbuf.shape[0]
    width = wbuf.shape[2]
    _, _, _, _, half, _ = full.shape
    rows = 2 * depth * 2 * half
    core, far, near, sibling, pair, line = position(gx_count)

    def load(c):
        return pltpu.make_async_copy(
            w_ref.at[pl.ds(pl.multiple_of(c * OUT_CHUNK, OUT_CHUNK), OUT_CHUNK), :], wbuf.at[c], wsem.at[c]
        )

    @pl.loop(0, chunks)
    def _(c):
        load(c).start()

    greet(sibling, pair, line, depth)
    give = remote(
        att_ref.at[1 - core],
        full.at[:, near, far, core],
        gsem.at[0],
        gsem.at[1],
        sibling,
    )
    give.start()

    @pl.loop(0, chunks)
    def _(c):
        full[c, near, far, core] = att_ref[core, c]

    acc[...] = jnp.zeros_like(acc)
    give.wait()

    def along(c, d):
        block = full.at[c, near, far]
        return remote(block, block, zs.at[c, d], zr.at[c, d], line(d))

    def across(c, d):
        block = full.at[c, near, lax.rem(far + depth - d, depth)]
        return remote(block, block, ys.at[c, d], yr.at[c, d], pair)

    ahead = 1
    lag = ahead + 1

    @pl.loop(0, chunks + lag)
    def _(c):
        @pl.when(c < chunks)
        def _():
            for d in range(depth - 1, 0, -1):
                along(c, d).start()
            across(c, 0).start()

        @pl.when((c >= ahead) & (c < chunks + ahead))
        def _():
            for d in range(1, depth):
                along(c - ahead, d).wait_recv()
                across(c - ahead, d).start()

        @pl.when(c >= lag)
        def _():
            cc = c - lag
            for d in range(depth):
                across(cc, d).wait_recv()
            load(cc).wait()
            acc[...] += jnp.dot(
                full[cc].reshape(rows, OUT_CHUNK), wbuf[cc], preferred_element_type=jnp.float32
            ).reshape(2, depth, 2 * half, width)

    keep = depth // 2
    last = remote(
        acc.at[:, pl.ds((1 - core) * keep, keep)], acc_in, fsem.at[0], fsem.at[1], sibling
    )
    last.start()

    @pl.loop(0, chunks)
    def _(c):
        across(c, 0).wait_send()
        for d in range(1, depth):
            along(c, d).wait_send()
            across(c, d).wait_send()

    last.wait()
    for z in range(keep):
        for y in range(2):
            out_ref[z, y] = (acc[y, core * keep + z] + acc_in[y, z]).astype(out_ref.dtype)


def output(attended, w_out, gx_count):
    _, chunks, half, _ = attended.shape
    width = w_out.shape[1]
    depth = gx_count // 2
    keep = depth // 2
    vmem = pl.BlockSpec(memory_space=pltpu.VMEM)
    dma = pltpu.SemaphoreType.DMA
    return pl.pallas_call(
        functools.partial(output_kernel, gx_count),
        out_shape=jax.ShapeDtypeStruct((keep, 2, 2 * half, width), jnp.bfloat16),
        in_specs=[vmem, pl.BlockSpec(memory_space=pl.ANY)],
        out_specs=vmem,
        scratch_shapes=[
            pltpu.VMEM((chunks, OUT_CHUNK, width), jnp.bfloat16),
            pltpu.VMEM((chunks, 2, depth, 2, half, OUT_CHUNK), jnp.bfloat16),
            pltpu.VMEM((2, depth, 2 * half, width), jnp.float32),
            pltpu.VMEM((2, keep, 2 * half, width), jnp.float32),
            dma((chunks,)),
            dma((2,)),
            dma((chunks, depth)),
            dma((chunks, depth)),
            dma((chunks, depth)),
            dma((chunks, depth)),
            dma((2,)),
        ],
        compiler_params=pltpu.CompilerParams(
            collective_id=2, has_side_effects=True, vmem_limit_bytes=56 * 1024 * 1024
        ),
    )(attended, w_out)


def attend_kernel(steps, lengths_ref, q_ref, kn_ref, vn_ref, k_ref, v_ref, out_ref):
    live = lengths_ref[pl.program_id(0)]
    total = k_ref.shape[1]
    block = total // 4
    for count in range(1, 5):

        @pl.when((live > (count - 1) * block) & (live <= count * block))
        def _():
            attend_slots(
                steps, count * block, live, q_ref, kn_ref, vn_ref, k_ref, v_ref, out_ref
            )


def attend_slots(steps, slots, live, q_ref, kn_ref, vn_ref, k_ref, v_ref, out_ref):
    kv_heads, queries, head_dim = q_ref.shape[1:]
    inverse = 1.0 / math.sqrt(head_dim)
    mask = lax.broadcasted_iota(jnp.int32, (queries, slots), 1) < live
    step = lax.broadcasted_iota(jnp.int32, (queries, 1), 0) // (queries // steps)
    heads = [slice(g * head_dim, (g + 1) * head_dim) for g in range(kv_heads)]
    mask = jnp.concatenate([mask] * kv_heads, axis=0)
    scores = [
        lax.dot_general(
            q_ref[0, g],
            k_ref[0, :slots, cols],
            (((1,), (1,)), ((), ())),
            preferred_element_type=jnp.float32,
        )
        for g, cols in enumerate(heads)
    ]
    scores = jnp.where(mask, jnp.concatenate(scores, axis=0) * inverse, -jnp.inf)
    highest = jnp.max(scores, axis=1, keepdims=True)
    fresh = []
    for s in range(steps):
        one = [
            jnp.sum(
                q_ref[0, g].astype(jnp.float32) * kn_ref[0, s : s + 1, cols].astype(jnp.float32),
                axis=1,
                keepdims=True,
            )
            * inverse
            for g, cols in enumerate(heads)
        ]
        one = jnp.concatenate([jnp.where(step >= s, part, -jnp.inf) for part in one], axis=0)
        highest = jnp.maximum(highest, one)
        fresh.append(one)
    exp_cache = jnp.exp(scores - highest)
    denominator = jnp.sum(exp_cache, axis=1, keepdims=True)
    exp_new = [jnp.exp(one - highest) for one in fresh]
    for one in exp_new:
        denominator = denominator + one
    scale = 1.0 / denominator
    weights = (exp_cache * scale).astype(jnp.bfloat16)
    new_weights = [(one * scale).astype(jnp.bfloat16).astype(jnp.float32) for one in exp_new]
    for g, cols in enumerate(heads):
        rows = slice(g * queries, (g + 1) * queries)
        result = jnp.dot(
            weights[rows, :], v_ref[0, :slots, cols], preferred_element_type=jnp.float32
        )
        for s in range(steps):
            result = result + new_weights[s][rows, :] * vn_ref[0, s : s + 1, cols].astype(
                jnp.float32
            )
        out_ref[0, g] = result.astype(jnp.bfloat16)


def attend(lengths, queries, keys_new, values_new, keys, values):
    rows, kv_heads, count, head_dim = queries.shape
    steps = keys_new.shape[1]
    slots, width = keys.shape[1:]
    return pl.pallas_call(
        functools.partial(attend_kernel, steps),
        out_shape=jax.ShapeDtypeStruct(queries.shape, jnp.bfloat16),
        grid_spec=pltpu.PrefetchScalarGridSpec(
            num_scalar_prefetch=1,
            grid=(rows,),
            in_specs=[
                pl.BlockSpec((1, kv_heads, count, head_dim), lambda r, _: (r, 0, 0, 0)),
                pl.BlockSpec((1, steps, width), lambda r, _: (r, 0, 0)),
                pl.BlockSpec((1, steps, width), lambda r, _: (r, 0, 0)),
                pl.BlockSpec((1, slots, width), lambda r, _: (r, 0, 0)),
                pl.BlockSpec((1, slots, width), lambda r, _: (r, 0, 0)),
            ],
            out_specs=pl.BlockSpec((1, kv_heads, count, head_dim), lambda r, _: (r, 0, 0, 0)),
        ),
        compiler_params=pltpu.CompilerParams(vmem_limit_bytes=56 * 1024 * 1024),
    )(lengths, queries, keys_new, values_new, keys, values)


def rotary_embed(inputs, token_positions):
    half_dim = inputs.shape[-1] // 2
    frequency = rope_base ** (-jnp.arange(half_dim, dtype=jnp.float32) / half_dim)
    angles = token_positions.astype(jnp.float32)[..., None, None] * frequency
    cosine = jnp.cos(angles)
    sine_part = jnp.sin(angles)
    lower_half = inputs[..., :half_dim]
    upper_half = inputs[..., half_dim:]
    return jnp.concatenate(
        [
            lower_half * cosine - upper_half * sine_part,
            upper_half * cosine + lower_half * sine_part,
        ],
        axis=-1,
    )


def local(
    hidden,
    norm_gain,
    w_query,
    key_weight,
    value_weight,
    w_out,
    stored_rotated_keys,
    stored_value_rows,
    lengths,
):
    gx_count = lax.axis_size("gx")
    gy_count = lax.axis_size("gy")
    steps, width = hidden.shape[1:]
    head_dim = HEAD_SIZE
    local_rows = lengths.shape[0]
    key_width = key_weight.shape[1]
    kv_heads = key_width * gy_count // head_dim
    mixed = project(
        hidden.reshape(-1, width),
        norm_gain.reshape(1, width),
        w_query,
        key_weight,
        value_weight,
        gx_count,
    )
    query_part = mixed[:, :-1]
    chunks = query_part.shape[1]
    per_chunk = CHUNK // head_dim
    queries = query_part.reshape(gy_count, chunks, local_rows, steps, per_chunk, head_dim)
    queries = queries.transpose(2, 3, 0, 1, 4, 5).reshape(local_rows, steps, -1, head_dim)
    fresh = mixed[:, -1].reshape(gy_count, local_rows, steps, 2, key_width).transpose(1, 2, 3, 0, 4)
    keys_new = fresh[:, :, 0].reshape(local_rows, steps, -1, head_dim)
    values_new = fresh[:, :, 1].reshape(local_rows, steps, -1)
    token_positions = lengths[:, None] + jnp.arange(steps)
    queries = rotary_embed(queries.astype(jnp.float32), token_positions).astype(jnp.bfloat16)
    keys_new = rotary_embed(keys_new.astype(jnp.float32), token_positions).astype(jnp.bfloat16)
    per_group = queries.shape[2] // kv_heads
    queries = queries.reshape(local_rows, steps, kv_heads, per_group, head_dim)
    queries = queries.transpose(0, 2, 1, 3, 4).reshape(
        local_rows, kv_heads, steps * per_group, head_dim
    )
    attended = attend(
        lengths,
        queries,
        keys_new.reshape(local_rows, steps, -1),
        values_new,
        stored_rotated_keys,
        stored_value_rows,
    )
    attended = attended.reshape(local_rows, gy_count, -1, steps, per_group * head_dim // OUT_CHUNK, OUT_CHUNK)
    attended = attended.transpose(1, 2, 4, 0, 3, 5).reshape(
        gy_count, -1, local_rows * steps, OUT_CHUNK
    )
    result = output(attended, w_out, gx_count)
    return result.reshape(-1, steps, width)


def solution(mesh):
    return jax.shard_map(
        local,
        mesh=mesh,
        in_specs=(
            P(("groups", "gy"), None, "gx"),
            P("gx"),
            P("gx", "gy"),
            P("gx", "gy"),
            P("gx", "gy"),
            P("gy", "gx"),
            P(("groups", "gx", "gy"), None, None),
            P(("groups", "gx", "gy"), None, None),
            P(("groups", "gx", "gy")),
        ),
        out_specs=P(("groups", "gy"), None, "gx"),
        check_vma=False,
    )
```
